256 devices in a mesh: seq: 64 (over x_hi, z, y), mp: 4 (over x_lo, core).
Axes of the slice: x: 4 (x_hi: 2, x_lo: 2; x = x_hi * 2 + x_lo), y: 4, z: 8, core: 2. Of those that a mesh axis runs over, the one named last changes fastest.
Arguments:
- queries: bfloat16 [16384, 1280], P('seq', 'mp'), may hold values from -77 to 77
- keys: bfloat16 [32768, 1280], P('seq', 'mp'), may hold values from -4 to 4
- values: bfloat16 [32768, 1280], P('seq', 'mp'), may hold values from -48 to 48
- out_weight: bfloat16 [1280, 1280], P('mp'), may hold values from -0.15625 to 0.15625
- grad_out: bfloat16 [16384, 1280], P('seq', 'mp'), may hold values from -24 to 24
- alignment: int32 [128, 2], P('seq'), may hold values from 0 to 256, as said below
Outputs:
- layer_output: bfloat16 [16384, 1280], P('seq', 'mp')
- query_grad: bfloat16 [16384, 1280], P('seq', 'mp')
- key_grad: bfloat16 [32768, 1280], P('seq', 'mp')
- value_grad: bfloat16 [32768, 1280], P('seq', 'mp')
The draws below stay inside these ranges and needn't reach their ends.
Inputs may be any that keep to these rules, and one draw needn't show every extreme that they name: Row g of alignment belongs to decoder block g, held by seq index i = g // 2. With k = 4: alignment[g, 0] < alignment[g, 1], max(0, (i - 1) * k) <= alignment[g, 0] <= i * k, and min(256, (i + 1) * k + 1) <= alignment[g, 1] <= min(256, (i + 3) * k).
All inputs are finite; a program needn't handle non-finite values.
Results may differ from the reference program's by a relative error of at most 0.012.
The reference program's roundings to bfloat16 on the way count: a program that leaves them out, or rounds other values in their place, can miss the bound.
Values may be sent and summed in bfloat16 or wider, within the bound.
No kernel may reach another device: no remote copies, remote signals or barrier semaphores. Data moves between devices by JAX's collectives and lax.ppermute only.
A program may use at most 64 MiB of HBM per device.

```python
import jax
import jax.numpy as jnp
from jax import lax

D = 1280
H = 20
DH = 64
BLK = 128
TQ = 256
TE = 512
NQ = 16384
NE = 32768
NQB = 128
NEB = 256
N_SEQ = 64


def base_pair(key):
    query_key = jax.random.fold_in(key, 31)
    frame_key = jax.random.fold_in(key, 32)
    raw_queries = jnp.clip(jax.random.normal(query_key, (NQ, H * DH), jnp.float32), -4.0, 4.0)
    raw_keys = jnp.clip(jax.random.normal(frame_key, (NE, H * DH), jnp.float32), -4.0, 4.0)
    return (raw_queries, raw_keys)


def draw_queries(key, part):
    raw_queries, raw_keys = base_pair(key)
    return raw_queries.astype(jnp.bfloat16)


def draw_keys(key, part):
    raw_queries, raw_keys = base_pair(key)
    return raw_keys.astype(jnp.bfloat16)


def draw_alignment(key, part):
    block_ids = jnp.arange(NQB, dtype=jnp.int32)
    frame_blocks = TE // BLK
    owner_index = block_ids // (TQ // BLK)
    window_first = (owner_index - 1) * frame_blocks
    lower_pick = jax.random.randint(jax.random.fold_in(key, 21), (NQB,), 0, frame_blocks + 1, dtype=jnp.int32)
    upper_pick = jax.random.randint(jax.random.fold_in(key, 22), (NQB,), 2 * frame_blocks + 1, 4 * frame_blocks + 1, dtype=jnp.int32)
    lower_block = jnp.clip(window_first + lower_pick, 0, NEB - 1)
    upper_block = jnp.clip(window_first + upper_pick, lower_block + 1, NEB)
    return jnp.stack([lower_block, upper_block], axis=1)


def block_levels(stream_key, dims, shards, smallest, high):
    def one(axis_at, shards_of):
        draws = jax.random.uniform(jax.random.fold_in(jax.random.fold_in(stream_key, 6), axis_at), (shards_of,), jnp.float32, smallest / len(shards), high / len(shards))
        return jnp.repeat(jnp.exp(draws), dims[axis_at] // shards_of).reshape((-1,) + (1,) * (len(dims) - axis_at - 1))

    factor_of = one(*shards[0])
    for cut in shards[1:]:
        factor_of = factor_of * one(*cut)
    return factor_of


def centred(key, dims, spread, most, split=(), held_as=jnp.bfloat16):
    factor_of = block_levels(key, dims, split, -0.22, 0.18) if split else 1.0
    values = jax.random.normal(key, dims, jnp.float32) * spread * factor_of
    return jnp.minimum(jnp.maximum(values, -most), most).astype(held_as)


def setup_inputs(seed: int = 0) -> dict:
    streams_of = jax.random.split(jax.random.key(seed), 7)
    queries = draw_queries(jax.random.fold_in(streams_of[6], 71), 0)
    keys = draw_keys(jax.random.fold_in(streams_of[6], 71), 0)
    values = centred(streams_of[2], (NE, H * DH), 8.0, 48.0, ((0, 64), (1, 4)))
    out_weight = centred(streams_of[3], (H * DH, D), D ** -0.5, 0.15625, ((0, 4),))
    grad_out = centred(streams_of[4], (NQ, D), 4.0, 24.0, ((0, 64), (1, 4)))
    alignment = draw_alignment(jax.random.fold_in(streams_of[6], 71), 0)
    return {"queries": queries, "keys": keys, "values": values, "out_weight": out_weight, "grad_out": grad_out, "alignment": alignment}


def dot_rows(first_op, second_op):
    return lax.dot_general(first_op, second_op, (((1,), (1,)), ((), ())), preferred_element_type=jnp.float32)


def dot_cols(first_op, second_op):
    return lax.dot_general(first_op, second_op, (((0,), (0,)), ((), ())), preferred_element_type=jnp.float32)


def allowed(key_blocks, ranges):
    lower_rows = jnp.repeat(ranges[:, 0], BLK)
    upper_rows = jnp.repeat(ranges[:, 1], BLK)
    return (key_blocks[None, :] >= lower_rows[:, None]) & (key_blocks[None, :] < upper_rows[:, None])


def reference(queries, keys, values, out_weight, grad_out, alignment):
    factor = DH ** -0.5
    feat_cols = H * DH
    frame_blocks = TE // BLK
    grad_attended = dot_rows(grad_out, out_weight).astype(jnp.bfloat16)
    pad_front = jnp.zeros((TE, feat_cols), jnp.bfloat16)
    pad_back = jnp.zeros((2 * TE, feat_cols), jnp.bfloat16)
    padded_keys = jnp.concatenate([pad_front, keys, pad_back], axis=0)
    padded_values = jnp.concatenate([pad_front, values, pad_back], axis=0)
    local_blocks = jnp.arange(4 * TE, dtype=jnp.int32) // BLK

    def one_device(carry, position):
        key_acc, value_acc = carry
        tok_start = position * TQ
        window_start = position * TE
        query_rows = lax.dynamic_slice_in_dim(queries, tok_start, TQ, 0)
        grad_rows = lax.dynamic_slice_in_dim(grad_attended, tok_start, TQ, 0)
        ranges = lax.dynamic_slice_in_dim(alignment, position * (TQ // BLK), TQ // BLK, 0)
        window_keys = lax.dynamic_slice_in_dim(padded_keys, window_start, 4 * TE, 0)
        window_values = lax.dynamic_slice_in_dim(padded_values, window_start, 4 * TE, 0)
        permit = allowed((position - 1) * frame_blocks + local_blocks, ranges)
        attended_parts, query_parts, key_parts, value_parts = [], [], [], []
        for head_index in range(H):
            columns = slice(head_index * DH, (head_index + 1) * DH)
            query_head = query_rows[:, columns]
            key_head = window_keys[:, columns]
            value_head = window_values[:, columns]
            grad_head = grad_rows[:, columns]
            scores = jnp.where(permit, dot_rows(query_head, key_head) * factor, -jnp.inf)
            top_score = jnp.max(scores, axis=1, keepdims=True)
            logsum = top_score + jnp.log(jnp.sum(jnp.exp(scores - top_score), axis=1, keepdims=True))
            prob_full = jnp.exp(scores - logsum)
            prob_low = prob_full.astype(jnp.bfloat16)
            attended = jnp.dot(prob_low, value_head, preferred_element_type=jnp.float32).astype(jnp.bfloat16)
            row_delta = jnp.sum(grad_head.astype(jnp.float32) * attended.astype(jnp.float32), axis=1, keepdims=True)
            dprobs = dot_rows(grad_head, value_head)
            dscores = (prob_full * (dprobs - row_delta) * factor).astype(jnp.bfloat16)
            query_parts.append(jnp.dot(dscores, key_head, preferred_element_type=jnp.float32).astype(jnp.bfloat16))
            key_parts.append(dot_cols(dscores, query_head))
            value_parts.append(dot_cols(prob_low, grad_head))
            attended_parts.append(attended)
        attended_all = jnp.concatenate(attended_parts, axis=1)
        key_window = jnp.concatenate(key_parts, axis=1)
        value_window = jnp.concatenate(value_parts, axis=1)
        key_acc = lax.dynamic_update_slice_in_dim(key_acc, lax.dynamic_slice_in_dim(key_acc, window_start, 4 * TE, 0) + key_window, window_start, 0)
        value_acc = lax.dynamic_update_slice_in_dim(value_acc, lax.dynamic_slice_in_dim(value_acc, window_start, 4 * TE, 0) + value_window, window_start, 0)
        output_rows = jnp.dot(attended_all, out_weight, preferred_element_type=jnp.float32).astype(jnp.bfloat16)
        return (key_acc, value_acc), (output_rows, jnp.concatenate(query_parts, axis=1))

    start_acc = jnp.zeros((NE + 3 * TE, feat_cols), jnp.float32)
    (key_acc, value_acc), (out_blocks, grad_blocks) = lax.scan(one_device, (start_acc, start_acc), jnp.arange(N_SEQ, dtype=jnp.int32))
    layer_output = out_blocks.reshape(NQ, D)
    query_grad = grad_blocks.reshape(NQ, feat_cols)
    key_grad = key_acc[TE:TE + NE].astype(jnp.bfloat16)
    value_grad = value_acc[TE:TE + NE].astype(jnp.bfloat16)
    return (layer_output, query_grad, key_grad, value_grad)
```

```python
import jax
import jax.numpy as jnp
from jax import lax
from jax.experimental import pallas as pl
from jax.experimental.pallas import tpu as pltpu
from jax.sharding import PartitionSpec as P

DH = 64
BLK = 128
PAIR = 2 * DH
LOG2E = 1.4426950408889634
NT = (((1,), (1,)), ((), ()))
NN = (((1,), (0,)), ((), ()))
VMEM = pl.BlockSpec(memory_space=pltpu.VMEM)
SMEM = pl.BlockSpec(memory_space=pltpu.SMEM)
PARAMS = pltpu.CompilerParams(vmem_limit_bytes=40 * 1024 * 1024)


def ring(value, by):
    count = lax.axis_size("seq")
    return lax.ppermute(value, "seq", [(i, (i + by) % count) for i in range(count)])


def dot(first_op, second_op, dims):
    return lax.dot_general(first_op, second_op, dims, preferred_element_type=jnp.float32)


def halves(pair):
    lane = lax.broadcasted_iota(jnp.int32, pair.shape, 1)
    zero = jnp.zeros_like(pair)
    return jnp.where(lane < DH, pair, zero), jnp.where(lane < DH, zero, pair)


def pack_frames(keys_ref, values_ref, out_ref):
    for head in range(out_ref.shape[0]):
        cols = slice(head * DH, (head + 1) * DH)
        out_ref[head] = jnp.concatenate([keys_ref[:, cols], values_ref[:, cols]], axis=1)


def pack_tokens(grad_ref, weight_ref, queries_ref, out_ref):
    grad = dot(grad_ref[...], weight_ref[...], NT).astype(jnp.bfloat16)
    for head in range(out_ref.shape[0]):
        cols = slice(head * DH, (head + 1) * DH)
        out_ref[head] = jnp.concatenate([queries_ref[:, cols], grad[:, cols]], axis=1)


def window_bias(rel_ref, frames, tokens):
    block = lax.broadcasted_iota(jnp.int32, (1, frames), 1) // BLK
    rows = [
        jnp.where((block >= rel_ref[g, 0]) & (block < rel_ref[g, 1]), 0.0, -jnp.inf).astype(
            jnp.float32
        )
        for g in range(tokens // BLK)
    ]
    return rows


def forward(
    rel_ref, align_ref, pair_ref, f0, f1, f2, f3, attended_ref, cols_ref, rows_ref, work
):
    heads, tokens, _ = pair_ref.shape
    slots = (f0, f1, f2, f3)
    span = f0.shape[1]
    scale = LOG2E * DH ** (-0.5)
    bias = window_bias(rel_ref, 4 * span, tokens)
    lane = lax.broadcasted_iota(jnp.int32, (tokens, 128), 1)
    row = lax.broadcasted_iota(jnp.int32, (tokens, 128), 0)
    lower = jnp.where(row < BLK, align_ref[0, 0], align_ref[1, 0]).astype(jnp.float32)
    upper = jnp.where(row < BLK, align_ref[0, 1], align_ref[1, 1]).astype(jnp.float32)
    stats = jnp.where(lane == 2 * heads, lower, jnp.where(lane == 2 * heads + 1, upper, 0.0))
    for head in range(heads):
        pair = pair_ref[head]
        query, _ = halves(pair)
        for g in range(tokens // BLK):
            rows = slice(g * BLK, (g + 1) * BLK)
            top = None
            for s, slot in enumerate(slots):
                raw = dot(query[rows], slot[head], NT) * scale + bias[g][:, s * span : (s + 1) * span]
                work[:, s * span : (s + 1) * span] = raw
                for c in range(0, span, 128):
                    part = raw[:, c : c + 128]
                    top = part if top is None else jnp.maximum(top, part)
            top = jnp.max(top, axis=1, keepdims=True)
            total = None
            for s in range(4):
                prob = jnp.exp2(work[:, s * span : (s + 1) * span] - top)
                work[:, s * span : (s + 1) * span] = prob
                for c in range(0, span, 128):
                    part = prob[:, c : c + 128]
                    total = part if total is None else total + part
            total = jnp.sum(total, axis=1, keepdims=True)
            inverse = 1.0 / total
            logsum = top + jnp.log2(total)
            out = None
            for s, slot in enumerate(slots):
                low = (work[:, s * span : (s + 1) * span] * inverse).astype(jnp.bfloat16)
                part = dot(low, slot[head], NN)
                out = part if out is None else out + part
            low_out = out.astype(jnp.bfloat16)
            attended_ref[rows, head * DH : (head + 1) * DH] = low_out[:, DH:]
            product = jnp.where(
                lane[rows] < DH, 0.0, low_out.astype(jnp.float32) * pair[rows].astype(jnp.float32)
            )
            delta = jnp.sum(product, axis=1, keepdims=True)
            part = stats[rows] if head == 0 else cols_ref[rows, :]
            part = jnp.where(lane[rows] == head, logsum, part)
            cols_ref[rows, :] = jnp.where(lane[rows] == heads + head, delta, part)
    rows_ref[...] = cols_ref[...].T[: rows_ref.shape[0]]


def query_side(rel_ref, pair_ref, cols_ref, f0, f1, f2, f3, grad_ref):
    heads, tokens, _ = pair_ref.shape
    slots = (f0, f1, f2, f3)
    span = f0.shape[1]
    factor = DH ** (-0.5)
    bias = window_bias(rel_ref, 4 * span, tokens)
    for head in range(heads):
        query, grad = halves(pair_ref[head])
        for g in range(tokens // BLK):
            rows = slice(g * BLK, (g + 1) * BLK)
            logsum = cols_ref[rows, head : head + 1]
            delta = cols_ref[rows, heads + head : heads + head + 1]
            out = None
            for s, slot in enumerate(slots):
                frame = slot[head]
                raw = dot(query[rows], frame, NT) * (LOG2E * factor)
                prob = jnp.exp2(raw + bias[g][:, s * span : (s + 1) * span] - logsum)
                dprob = dot(grad[rows], frame, NT)
                low = (prob * (dprob - delta)).astype(jnp.bfloat16)
                part = dot(low, frame, NN)
                out = part if out is None else out + part
            grad_ref[rows, head * DH : (head + 1) * DH] = (out[:, :DH] * factor).astype(jnp.bfloat16)


def frame_side(
    place_ref, own_ref, p0, p1, p2, p3, s0, s1, s2, s3, key_grad_ref, value_grad_ref
):
    heads, span, _ = own_ref.shape
    tokens = p0.shape[1]
    factor = DH ** (-0.5)
    first = place_ref[0]
    sources = ((p0, s0), (p1, s1), (p2, s2), (p3, s3))
    bias = []
    for _, stat in sources:
        lower, upper = (stat[2 * heads : 2 * heads + 1, :], stat[2 * heads + 1 : 2 * heads + 2, :])
        per = []
        for b in range(span // BLK):
            block = (first + b).astype(jnp.float32)
            per.append(jnp.where((lower <= block) & (block < upper), 0.0, -jnp.inf))
        bias.append(per)
    for head in range(heads):
        frame = own_ref[head]
        out = None
        for j, (pair_ref, stat) in enumerate(sources):
            both = jnp.concatenate(halves(pair_ref[head]), axis=0)
            logsum = stat[head : head + 1, :]
            delta = stat[heads + head : heads + head + 1, :]
            raw = dot(frame, both, NT)
            lows = []
            for b in range(span // BLK):
                rows = slice(b * BLK, (b + 1) * BLK)
                prob = jnp.exp2(raw[rows, :tokens] * (LOG2E * factor) + (bias[j][b] - logsum))
                dscore = prob * (raw[rows, tokens:] - delta)
                lows.append(
                    jnp.concatenate(
                        [dscore.astype(jnp.bfloat16), prob.astype(jnp.bfloat16)], axis=1
                    )
                )
            part = dot(jnp.concatenate(lows, axis=0), both, NN)
            out = part if out is None else out + part
        cols = slice(head * DH, (head + 1) * DH)
        key_grad_ref[:, cols] = (out[:, :DH] * factor).astype(jnp.bfloat16)
        value_grad_ref[:, cols] = out[:, DH:].astype(jnp.bfloat16)


def after(value, *others):
    return lax.optimization_barrier((value,) + others)[0]


def on_device(queries, keys, values, out_weight, grad_out, alignment):
    frames, feats = keys.shape
    tokens = queries.shape[0]
    heads = feats // DH
    frame_blocks = frames // BLK
    position = lax.axis_index("seq").astype(jnp.int32)
    shape = jax.ShapeDtypeStruct
    bf16, f32 = jnp.bfloat16, jnp.float32

    with jax.named_scope("pack_frames"):
        frame_pack = pl.pallas_call(
            pack_frames,
            out_shape=shape((heads, frames, PAIR), bf16),
            in_specs=[VMEM] * 2,
            out_specs=VMEM,
            compiler_params=PARAMS,
        )(keys, values)
    window = [ring(frame_pack, 1), frame_pack, ring(frame_pack, -1), ring(frame_pack, -2)]

    grad_all = lax.all_gather(grad_out, "mp", axis=1, tiled=True)
    with jax.named_scope("pack_tokens"):
        token_pack = pl.pallas_call(
            pack_tokens,
            out_shape=shape((heads, tokens, PAIR), bf16),
            in_specs=[VMEM] * 3,
            out_specs=VMEM,
            compiler_params=PARAMS,
        )(grad_all, out_weight, queries)
    weight_cols = lax.all_to_all(out_weight, "mp", 1, 0, tiled=True)

    sent_pack = after(token_pack, *window)
    token_packs = [ring(sent_pack, 1), ring(sent_pack, -1), ring(sent_pack, 2)]

    relative = alignment - (position - 1) * frame_blocks
    with jax.named_scope("forward"):
        attended, stat_cols, stat_rows = pl.pallas_call(
            forward,
            out_shape=(
                shape((tokens, feats), bf16),
                shape((tokens, 128), f32),
                shape((16, tokens), f32),
            ),
            in_specs=[SMEM] * 2 + [VMEM] * 5,
            out_specs=(VMEM,) * 3,
            scratch_shapes=[pltpu.VMEM((BLK, 4 * frames), f32)],
            compiler_params=PARAMS,
        )(relative, alignment, token_pack, *window)
    stats = [ring(stat_rows, 1), ring(stat_rows, -1), ring(stat_rows, 2)]

    attended_all = lax.all_gather(attended, "mp", axis=1, tiled=True)
    layer_output = dot(attended_all, weight_cols, NN).astype(bf16)

    with jax.named_scope("query_side"):
        query_grad = pl.pallas_call(
            query_side,
            out_shape=shape((tokens, feats), bf16),
            in_specs=[SMEM] + [VMEM] * 6,
            out_specs=VMEM,
            compiler_params=PARAMS,
        )(relative, token_pack, stat_cols, *window)

    with jax.named_scope("frame_side"):
        key_grad, value_grad = pl.pallas_call(
            frame_side,
            out_shape=(shape((frames, feats), bf16),) * 2,
            in_specs=[SMEM] + [VMEM] * 9,
            out_specs=(VMEM,) * 2,
            compiler_params=PARAMS,
        )(
            (position * frame_blocks).reshape(1),
            frame_pack,
            token_pack,
            *token_packs,
            stat_rows,
            *stats,
        )
    return layer_output, query_grad, key_grad, value_grad


def solution(mesh):
    return jax.shard_map(
        on_device,
        mesh=mesh,
        in_specs=(
            P("seq", "mp"),
            P("seq", "mp"),
            P("seq", "mp"),
            P("mp", None),
            P("seq", "mp"),
            P("seq", None),
        ),
        out_specs=(P("seq", "mp"), P("seq", "mp"), P("seq", "mp"), P("seq", "mp")),
        check_vma=False,
    )
```

```python
import jax
import jax.numpy as jnp
from jax import lax
from jax.experimental import pallas as pl
from jax.experimental.pallas import tpu as pltpu
from jax.sharding import PartitionSpec as P

DH = 64
BLK = 128
PAIR = 2 * DH
FACTOR = DH ** (-0.5)
LOG2E = 1.4426950408889634
FAR = -1e30
BIAS_ROWS = 16
TERMS = 3
STAT_ROWS = 16
NT = (((1,), (1,)), ((), ()))
NN = (((1,), (0,)), ((), ()))
VMEM = pl.BlockSpec(memory_space=pltpu.VMEM)
SMEM = pl.BlockSpec(memory_space=pltpu.SMEM)
HBM = pl.BlockSpec(memory_space=pltpu.HBM)
PARAMS = pltpu.CompilerParams(vmem_limit_bytes=20 * 1024 * 1024)


def ring(value, by):
    count = lax.axis_size("seq")
    return lax.ppermute(value, "seq", [(i, (i + by) % count) for i in range(count)])


def dot(first_op, second_op, dims):
    return lax.dot_general(first_op, second_op, dims, preferred_element_type=jnp.float32)


def iota(shape, dim):
    return lax.broadcasted_iota(jnp.int32, shape, dim)


def pack_frames(keys_ref, values_ref, out_ref, done):
    copies = []
    for head in range(out_ref.shape[0]):
        rows = pl.ds(head * DH, DH)
        for side, source in enumerate((keys_ref, values_ref)):
            target = out_ref.at[head, pl.ds(side * DH, DH)]
            copies.append(pltpu.make_async_copy(source.at[rows], target, done.at[side, head]))
    for copy in copies:
        copy.start()
    for copy in copies:
        copy.wait()


def pack_tokens(me_ref, own_ref, far_ref, other_ref, weight_ref, queries_ref, out_ref, whole):
    feats = own_ref.shape[0]
    parts = (own_ref[...], far_ref[...], other_ref[:feats], other_ref[feats:])
    for part, flip in zip(parts, (0, 2, 1, 3)):
        first = pl.multiple_of((me_ref[0] ^ flip) * feats, feats)
        whole[pl.ds(first, feats), :] = part
    grad = dot(weight_ref[...], whole[...], NN).astype(jnp.bfloat16)
    for head in range(out_ref.shape[0]):
        rows = slice(head * DH, (head + 1) * DH)
        out_ref[head, :DH] = queries_ref[rows]
        out_ref[head, DH:] = grad[rows]


def three_terms(row):
    high = row.astype(jnp.bfloat16).astype(jnp.float32)
    middle = (row - high).astype(jnp.bfloat16).astype(jnp.float32)
    return [high, middle, row - high - middle]


def padded(parts):
    have = sum(p.shape[0] for p in parts)
    zeros = jnp.zeros((DH - have, parts[0].shape[1]), jnp.float32)
    return jnp.concatenate(parts + [zeros], axis=0).astype(jnp.bfloat16)


def turned(parts):
    return jnp.concatenate(parts, axis=0).T


def block_bias(first_block, lower, upper):
    block = (first_block + iota((BIAS_ROWS, lower.shape[1]), 0)).astype(jnp.float32)
    return jnp.where((lower <= block) & (block < upper), 0.0, FAR)


def score_rows(frames, first_row):
    row = iota((DH, frames), 0)
    block = first_row + iota((DH, frames), 1) // BLK
    ones = jnp.where(row == block, 1.0, 0.0)
    minus = (row >= BIAS_ROWS) & (row < BIAS_ROWS + TERMS)
    return jnp.where(minus, -1.0, ones).astype(jnp.bfloat16)


def dprob_rows(frames):
    return jnp.where(iota((DH, frames), 0) < TERMS, -1.0, 0.0).astype(jnp.bfloat16)


def score_side(pair, bias, logsum):
    return turned([pair[:DH], padded([bias] + three_terms(logsum))])


def dprob_side(pair, delta):
    return turned([padded(three_terms(delta)), pair[DH:]])


def forward(place_ref, align_ref, pair_ref, f0, f1, f2, f3, attended_ref, stats_ref, work, sums):
    heads, _, tokens = pair_ref.shape
    slots = (f0, f1, f2, f3)
    span = f0.shape[2]
    lane = iota((1, tokens), 1)
    lower = jnp.where(lane < BLK, align_ref[0, 0], align_ref[1, 0]).astype(jnp.float32)
    upper = jnp.where(lane < BLK, align_ref[0, 1], align_ref[1, 1]).astype(jnp.float32)
    bias = block_bias(place_ref[0] - span // BLK, lower, upper)
    beside = [score_rows(span, s * (span // BLK)) for s in range(4)]
    units = [(head, g) for head in range(heads) for g in range(tokens // BLK)]
    sides = {}

    def scores(unit):
        head, g = units[unit]
        if g == 0:
            sides[head] = turned([pair_ref[head, :DH], padded([bias])])
        left = sides[head][g * BLK : (g + 1) * BLK]
        top = None
        for s, slot in enumerate(slots):
            raw = dot(left, jnp.concatenate([slot[head, :DH], beside[s]], axis=0), NN)
            work[unit % 3, :, s * span : (s + 1) * span] = raw
            for c in range(0, span, 128):
                part = raw[:, c : c + 128]
                top = part if top is None else jnp.maximum(top, part)
        return jnp.max(top, axis=1, keepdims=True)

    ahead = scores(0)
    for unit, (head, g) in enumerate(units):
        top = ahead
        if unit + 1 < len(units):
            ahead = scores(unit + 1)
        total = None
        for s in range(4):
            raw = work[unit % 3, :, s * span : (s + 1) * span]
            prob = jnp.exp2((raw - top) * (LOG2E * FACTOR))
            work[unit % 3, :, s * span : (s + 1) * span] = prob
            for c in range(0, span, 128):
                part = prob[:, c : c + 128]
                total = part if total is None else total + part
        total = jnp.sum(total, axis=1, keepdims=True)
        inverse = 1.0 / total
        cols = slice(g * BLK, (g + 1) * BLK)
        sums[cols, head : head + 1] = top + jnp.log(total) * (1.0 / FACTOR)
        out = None
        for s, slot in enumerate(slots):
            low = (work[unit % 3, :, s * span : (s + 1) * span] * inverse).astype(jnp.bfloat16)
            part = dot(low, slot[head, DH:], NT)
            out = part if out is None else out + part
        low_out = out.T.astype(jnp.bfloat16)
        attended_ref[head * DH : (head + 1) * DH, cols] = low_out
        product = low_out.astype(jnp.float32) * pair_ref[head, DH:, cols].astype(jnp.float32)
        stats_ref[heads + head : heads + head + 1, cols] = jnp.sum(product, axis=0, keepdims=True)
    stats_ref[:heads, :] = sums[...].T[:heads]
    stats_ref[2 * heads : 2 * heads + 1, :] = lower
    stats_ref[2 * heads + 1 : 2 * heads + 2, :] = upper
    stats_ref[2 * heads + 2 :, :] = jnp.zeros((STAT_ROWS - 2 * heads - 2, tokens), jnp.float32)


def stat_rows(stats_ref, heads, head):
    return stats_ref[head : head + 1, :], stats_ref[heads + head : heads + head + 1, :]


def span_bias(stats_ref, heads, first_block):
    lower, upper = stats_ref[2 * heads : 2 * heads + 1, :], stats_ref[2 * heads + 1 : 2 * heads + 2, :]
    return block_bias(first_block, lower, upper)


def query_side(place_ref, pair_ref, stats_ref, f0, f1, f2, f3, grad_ref):
    heads, _, tokens = pair_ref.shape
    slots = (f0, f1, f2, f3)
    span = f0.shape[2]
    bias = span_bias(stats_ref, heads, place_ref[0] - span // BLK)
    beside = [score_rows(span, s * (span // BLK)) for s in range(4)]
    above = dprob_rows(span)
    units = [(head, s) for head in range(heads) for s in range(4)]
    sides = {}

    def products(unit):
        head, s = units[unit]
        if s == 0:
            pair = pair_ref[head]
            logsum, delta = stat_rows(stats_ref, heads, head)
            sides[head] = score_side(pair, bias, logsum), dprob_side(pair, delta)
        left, grad_left = sides[head]
        raw = dot(left, jnp.concatenate([slots[s][head, :DH], beside[s]], axis=0), NN)
        return raw, dot(grad_left, jnp.concatenate([above, slots[s][head, DH:]], axis=0), NN)

    ahead = products(0)
    out = None
    for unit, (head, s) in enumerate(units):
        raw, dprob = ahead
        if unit + 1 < len(units):
            ahead = products(unit + 1)
        low = (jnp.exp2(raw * (LOG2E * FACTOR)) * dprob).astype(jnp.bfloat16)
        part = dot(slots[s][head, :DH], low, NT)
        out = part if s == 0 else out + part
        if s == 3:
            rows = slice(head * DH, (head + 1) * DH)
            grad_ref[rows, :] = (out * FACTOR).astype(jnp.bfloat16)


def frame_side(
    place_ref, own_ref, p0, p1, p2, p3, s0, s1, s2, s3, key_grad_ref, value_grad_ref
):
    heads, _, span = own_ref.shape
    sources = ((p0, s0), (p1, s1), (p2, s2), (p3, s3))
    bias = [span_bias(stats, heads, place_ref[0]) for _, stats in sources]
    beside = score_rows(span, 0)
    above = dprob_rows(span)
    units = [(head, j) for head in range(heads) for j in range(len(sources))]

    def products(unit):
        head, j = units[unit]
        right = jnp.concatenate([own_ref[head, :DH], beside], axis=0)
        grad_right = jnp.concatenate([above, own_ref[head, DH:]], axis=0)
        pair = sources[j][0][head]
        logsum, delta = stat_rows(sources[j][1], heads, head)
        raw = dot(score_side(pair, bias[j], logsum), right, NN)
        return raw, dot(dprob_side(pair, delta), grad_right, NN)

    ahead = products(0)
    key_out, value_out = None, None
    for unit, (head, j) in enumerate(units):
        raw, dprob = ahead
        if unit + 1 < len(units):
            ahead = products(unit + 1)
        pair_ref = sources[j][0]
        prob = jnp.exp2(raw * (LOG2E * FACTOR))
        key_part = dot(pair_ref[head, :DH], (prob * dprob).astype(jnp.bfloat16), NN)
        value_part = dot(pair_ref[head, DH:], prob.astype(jnp.bfloat16), NN)
        key_out = key_part if j == 0 else key_out + key_part
        value_out = value_part if j == 0 else value_out + value_part
        if j == len(sources) - 1:
            rows = slice(head * DH, (head + 1) * DH)
            key_grad_ref[rows, :] = (key_out * FACTOR).astype(jnp.bfloat16)
            value_grad_ref[rows, :] = value_out.astype(jnp.bfloat16)


def project(me_ref, weight_ref, attended_ref, kept_ref, sent_ref, whole):
    feats = attended_ref.shape[0]
    whole[...] = dot(weight_ref[...], attended_ref[...], NN)
    for place, flip in enumerate((0, 1)):
        block = pl.ds(pl.multiple_of((me_ref[0] ^ flip) * feats, feats), feats)
        kept_ref[place] = whole[block, :]
    for place, flip in enumerate((2, 3)):
        block = pl.ds(pl.multiple_of((me_ref[0] ^ flip) * feats, feats), feats)
        sent_ref[place] = whole[block, :].astype(jnp.bfloat16)


def after(value, *others):
    return lax.optimization_barrier((value,) + others)[0]


def call(kernel, outs, specs, *operands, scratch=(), steps=0):
    many = isinstance(outs, tuple)
    cost = pl.CostEstimate(flops=steps * 4_000_000_000, bytes_accessed=0, transcendentals=0)
    with jax.named_scope(kernel.__name__):
        return pl.pallas_call(
            kernel,
            out_shape=outs,
            in_specs=specs,
            out_specs=(VMEM,) * len(outs) if many else VMEM,
            scratch_shapes=scratch,
            compiler_params=PARAMS,
            cost_estimate=cost if steps else None,
        )(*operands)


def flipped(value, by):
    return lax.ppermute(value, "mp", [(i, i ^ by) for i in range(lax.axis_size("mp"))])


def on_device(queries, keys, values, out_weight, grad_out, alignment):
    queries, keys, values, grad_out = queries.T, keys.T, values.T, grad_out.T
    feats, frames = keys.shape
    tokens = queries.shape[1]
    heads = feats // DH
    me = lax.axis_index("mp").astype(jnp.int32).reshape(1)
    place = (lax.axis_index("seq").astype(jnp.int32) * (frames // BLK)).reshape(1)
    bf16, f32 = jnp.bfloat16, jnp.float32
    shape = jax.ShapeDtypeStruct

    grad_far = flipped(grad_out, 2)
    frame_pack = call(
        pack_frames,
        shape((heads, PAIR, frames), bf16),
        [HBM] * 2,
        keys,
        values,
        scratch=[pltpu.SemaphoreType.DMA((2, heads))],
    )
    grad_own = after(grad_out, frame_pack)
    grad_other = flipped(jnp.concatenate([grad_own, grad_far], axis=0), 1)
    later_pack = after(frame_pack, grad_far)
    window = [ring(later_pack, 1), frame_pack, ring(later_pack, -1), ring(frame_pack, -2)]

    token_pack = call(
        pack_tokens,
        shape((heads, PAIR, tokens), bf16),
        [SMEM] + [VMEM] * 5,
        me,
        grad_own,
        grad_far,
        grad_other,
        out_weight,
        queries,
        scratch=[pltpu.VMEM((4 * feats, tokens), bf16)],
    )
    turned_weight = after(out_weight, token_pack).T
    token_packs = [
        ring(token_pack, 1),
        ring(token_pack, -1),
        ring(after(token_pack, window[3]), 2),
    ]

    attended, stats = call(
        forward,
        (shape((feats, tokens), bf16), shape((STAT_ROWS, tokens), f32)),
        [SMEM] * 2 + [VMEM] * 5,
        place,
        after(alignment, turned_weight),
        token_pack,
        *window,
        scratch=[pltpu.VMEM((3, BLK, 4 * frames), f32), pltpu.VMEM((tokens, 128), f32)],
        steps=1,
    )
    sent_stats = after(stats, *token_packs)
    near_stats = [ring(sent_stats, 1), ring(sent_stats, -1), ring(sent_stats, 2)]

    kept, sent = call(
        project,
        (shape((2, feats, tokens), f32), shape((2, feats, tokens), bf16)),
        [SMEM] + [VMEM] * 2,
        me,
        turned_weight,
        attended,
        scratch=[pltpu.VMEM((4 * feats, tokens), f32)],
    )
    kept = kept + flipped(sent, 2).astype(f32)
    layer_output = (kept[0] + flipped(kept[1].astype(bf16), 1).astype(f32)).astype(bf16)
    query_grad = call(
        query_side,
        shape((feats, tokens), bf16),
        [SMEM] + [VMEM] * 6,
        place,
        token_pack,
        sent_stats,
        *window,
        steps=1,
    )
    key_grad, value_grad = call(
        frame_side,
        (shape((feats, frames), bf16),) * 2,
        [SMEM] + [VMEM] * 9,
        place,
        frame_pack,
        token_pack,
        *token_packs,
        after(sent_stats, layer_output, query_grad),
        *near_stats,
        steps=1,
    )
    return layer_output.T, query_grad.T, key_grad.T, value_grad.T


def solution(mesh):
    return jax.shard_map(
        on_device,
        mesh=mesh,
        in_specs=(
            P("seq", "mp"),
            P("seq", "mp"),
            P("seq", "mp"),
            P("mp", None),
            P("seq", "mp"),
            P("seq", None),
        ),
        out_specs=(P("seq", "mp"), P("seq", "mp"), P("seq", "mp"), P("seq", "mp")),
        check_vma=False,
    )
```

```python
import jax
import jax.numpy as jnp
from jax import lax
from jax.experimental import pallas as pl
from jax.experimental.pallas import tpu as pltpu
from jax.sharding import PartitionSpec as P

DH = 64
BLK = 128
PAIR = 2 * DH
FACTOR = DH ** (-0.5)
LOG2E = 1.4426950408889634
FAR = -1e30
BIAS_ROWS = 16
TERMS = 3
STAT_ROWS = 16
NT = (((1,), (1,)), ((), ()))
NN = (((1,), (0,)), ((), ()))
VMEM = pl.BlockSpec(memory_space=pltpu.VMEM)
SMEM = pl.BlockSpec(memory_space=pltpu.SMEM)
HBM = pl.BlockSpec(memory_space=pltpu.HBM)
PARAMS = pltpu.CompilerParams(vmem_limit_bytes=20 * 1024 * 1024)


def ring(value, by):
    count = lax.axis_size("seq")
    return lax.ppermute(value, "seq", [(i, (i + by) % count) for i in range(count)])


def dot(first_op, second_op, dims):
    return lax.dot_general(first_op, second_op, dims, preferred_element_type=jnp.float32)


def iota(shape, dim):
    return lax.broadcasted_iota(jnp.int32, shape, dim)


def pack_frames(keys_ref, values_ref, out_ref, done):
    copies = []
    for head in range(out_ref.shape[0]):
        rows = pl.ds(head * DH, DH)
        for side, source in enumerate((keys_ref, values_ref)):
            target = out_ref.at[head, pl.ds(side * DH, DH)]
            copies.append(pltpu.make_async_copy(source.at[rows], target, done.at[side, head]))
    for copy in copies:
        copy.start()
    for copy in copies:
        copy.wait()


def pack_tokens(me_ref, own_ref, far_ref, other_ref, weight_ref, queries_ref, out_ref, whole):
    feats = own_ref.shape[0]
    parts = (own_ref[...], far_ref[...], other_ref[:feats], other_ref[feats:])
    for part, flip in zip(parts, (0, 2, 1, 3)):
        first = pl.multiple_of((me_ref[0] ^ flip) * feats, feats)
        whole[pl.ds(first, feats), :] = part
    grad = dot(weight_ref[...], whole[...], NN).astype(jnp.bfloat16)
    for head in range(out_ref.shape[0]):
        rows = slice(head * DH, (head + 1) * DH)
        out_ref[head, :DH] = queries_ref[rows]
        out_ref[head, DH:] = grad[rows]


def three_terms(row):
    high = row.astype(jnp.bfloat16).astype(jnp.float32)
    middle = (row - high).astype(jnp.bfloat16).astype(jnp.float32)
    return [high, middle, row - high - middle]


def padded(parts):
    have = sum(p.shape[0] for p in parts)
    zeros = jnp.zeros((DH - have, parts[0].shape[1]), jnp.float32)
    return jnp.concatenate(parts + [zeros], axis=0).astype(jnp.bfloat16)


def turned(parts):
    return jnp.concatenate(parts, axis=0).T


def block_bias(first_block, lower, upper):
    block = (first_block + iota((BIAS_ROWS, lower.shape[1]), 0)).astype(jnp.float32)
    return jnp.where((lower <= block) & (block < upper), 0.0, FAR)


def score_rows(frames, first_row):
    row = iota((DH, frames), 0)
    block = first_row + iota((DH, frames), 1) // BLK
    ones = jnp.where(row == block, 1.0, 0.0)
    minus = (row >= BIAS_ROWS) & (row < BIAS_ROWS + TERMS)
    return jnp.where(minus, -1.0, ones).astype(jnp.bfloat16)


def dprob_rows(frames):
    return jnp.where(iota((DH, frames), 0) < TERMS, -1.0, 0.0).astype(jnp.bfloat16)


def score_side(pair, bias, logsum):
    return turned([pair[:DH], padded([bias] + three_terms(logsum))])


def dprob_side(pair, delta):
    return turned([padded(three_terms(delta)), pair[DH:]])


def forward(place_ref, align_ref, pair_ref, f0, f1, f2, f3, attended_ref, stats_ref, work, sums):
    heads, _, tokens = pair_ref.shape
    slots = (f0, f1, f2, f3)
    span = f0.shape[2]
    lane = iota((1, tokens), 1)
    lower = jnp.where(lane < BLK, align_ref[0, 0], align_ref[1, 0]).astype(jnp.float32)
    upper = jnp.where(lane < BLK, align_ref[0, 1], align_ref[1, 1]).astype(jnp.float32)
    bias = block_bias(place_ref[0] - span // BLK, lower, upper)
    beside = [score_rows(span, s * (span // BLK)) for s in range(4)]
    units = [(head, g) for head in range(heads) for g in range(tokens // BLK)]
    sides = {}

    def scores(unit):
        head, g = units[unit]
        if g == 0:
            sides[head] = turned([pair_ref[head, :DH], padded([bias])])
        left = sides[head][g * BLK : (g + 1) * BLK]
        top = None
        for s, slot in enumerate(slots):
            raw = dot(left, jnp.concatenate([slot[head, :DH], beside[s]], axis=0), NN)
            work[unit % 3, :, s * span : (s + 1) * span] = raw
            for c in range(0, span, 128):
                part = raw[:, c : c + 128]
                top = part if top is None else jnp.maximum(top, part)
        return jnp.max(top, axis=1, keepdims=True)

    ahead = scores(0)
    for unit, (head, g) in enumerate(units):
        top = ahead
        if unit + 1 < len(units):
            ahead = scores(unit + 1)
        total = None
        for s in range(4):
            raw = work[unit % 3, :, s * span : (s + 1) * span]
            prob = jnp.exp2((raw - top) * (LOG2E * FACTOR))
            work[unit % 3, :, s * span : (s + 1) * span] = prob
            for c in range(0, span, 128):
                part = prob[:, c : c + 128]
                total = part if total is None else total + part
        total = jnp.sum(total, axis=1, keepdims=True)
        inverse = 1.0 / total
        cols = slice(g * BLK, (g + 1) * BLK)
        sums[cols, head : head + 1] = top + jnp.log(total) * (1.0 / FACTOR)
        out = None
        for s, slot in enumerate(slots):
            low = (work[unit % 3, :, s * span : (s + 1) * span] * inverse).astype(jnp.bfloat16)
            part = dot(low, slot[head, DH:], NT)
            out = part if out is None else out + part
        low_out = out.T.astype(jnp.bfloat16)
        attended_ref[head * DH : (head + 1) * DH, cols] = low_out
        product = low_out.astype(jnp.float32) * pair_ref[head, DH:, cols].astype(jnp.float32)
        stats_ref[heads + head : heads + head + 1, cols] = jnp.sum(product, axis=0, keepdims=True)
    stats_ref[:heads, :] = sums[...].T[:heads]
    stats_ref[2 * heads : 2 * heads + 1, :] = lower
    stats_ref[2 * heads + 1 : 2 * heads + 2, :] = upper
    stats_ref[2 * heads + 2 :, :] = jnp.zeros((STAT_ROWS - 2 * heads - 2, tokens), jnp.float32)


def stat_rows(stats_ref, heads, head):
    return stats_ref[head : head + 1, :], stats_ref[heads + head : heads + head + 1, :]


def span_bias(stats_ref, heads, first_block):
    lower, upper = stats_ref[2 * heads : 2 * heads + 1, :], stats_ref[2 * heads + 1 : 2 * heads + 2, :]
    return block_bias(first_block, lower, upper)


def query_side(place_ref, pair_ref, stats_ref, f0, f1, f2, f3, grad_ref):
    heads, _, tokens = pair_ref.shape
    slots = (f0, f1, f2, f3)
    span = f0.shape[2]
    bias = span_bias(stats_ref, heads, place_ref[0] - span // BLK)
    beside = [score_rows(span, s * (span // BLK)) for s in range(4)]
    above = dprob_rows(span)
    units = [(head, s) for head in range(heads) for s in range(4)]
    sides = {}

    def products(unit):
        head, s = units[unit]
        if s == 0:
            pair = pair_ref[head]
            logsum, delta = stat_rows(stats_ref, heads, head)
            sides[head] = score_side(pair, bias, logsum), dprob_side(pair, delta)
        left, grad_left = sides[head]
        raw = dot(left, jnp.concatenate([slots[s][head, :DH], beside[s]], axis=0), NN)
        return raw, dot(grad_left, jnp.concatenate([above, slots[s][head, DH:]], axis=0), NN)

    ahead = products(0)
    out = None
    for unit, (head, s) in enumerate(units):
        raw, dprob = ahead
        if unit + 1 < len(units):
            ahead = products(unit + 1)
        low = (jnp.exp2(raw * (LOG2E * FACTOR)) * dprob).astype(jnp.bfloat16)
        part = dot(slots[s][head, :DH], low, NT)
        out = part if s == 0 else out + part
        if s == 3:
            rows = slice(head * DH, (head + 1) * DH)
            grad_ref[rows, :] = (out * FACTOR).astype(jnp.bfloat16)


def frame_side(
    place_ref, own_ref, p0, p1, p2, p3, s0, s1, s2, s3, key_grad_ref, value_grad_ref
):
    heads, _, span = own_ref.shape
    sources = ((p0, s0), (p1, s1), (p2, s2), (p3, s3))
    bias = [span_bias(stats, heads, place_ref[0]) for _, stats in sources]
    beside = score_rows(span, 0)
    above = dprob_rows(span)
    units = [(head, j) for head in range(heads) for j in range(len(sources))]

    def products(unit):
        head, j = units[unit]
        right = jnp.concatenate([own_ref[head, :DH], beside], axis=0)
        grad_right = jnp.concatenate([above, own_ref[head, DH:]], axis=0)
        pair = sources[j][0][head]
        logsum, delta = stat_rows(sources[j][1], heads, head)
        raw = dot(score_side(pair, bias[j], logsum), right, NN)
        return raw, dot(dprob_side(pair, delta), grad_right, NN)

    ahead = products(0)
    key_out, value_out = None, None
    for unit, (head, j) in enumerate(units):
        raw, dprob = ahead
        if unit + 1 < len(units):
            ahead = products(unit + 1)
        pair_ref = sources[j][0]
        prob = jnp.exp2(raw * (LOG2E * FACTOR))
        key_part = dot(pair_ref[head, :DH], (prob * dprob).astype(jnp.bfloat16), NN)
        value_part = dot(pair_ref[head, DH:], prob.astype(jnp.bfloat16), NN)
        key_out = key_part if j == 0 else key_out + key_part
        value_out = value_part if j == 0 else value_out + value_part
        if j == len(sources) - 1:
            rows = slice(head * DH, (head + 1) * DH)
            key_grad_ref[rows, :] = (key_out * FACTOR).astype(jnp.bfloat16)
            value_grad_ref[rows, :] = value_out.astype(jnp.bfloat16)


def project(me_ref, weight_ref, attended_ref, kept_ref, sent_ref, whole):
    feats = attended_ref.shape[0]
    whole[...] = dot(weight_ref[...], attended_ref[...], NN)
    for place, flip in enumerate((0, 1)):
        block = pl.ds(pl.multiple_of((me_ref[0] ^ flip) * feats, feats), feats)
        kept_ref[place] = whole[block, :]
    for place, flip in enumerate((2, 3)):
        block = pl.ds(pl.multiple_of((me_ref[0] ^ flip) * feats, feats), feats)
        sent_ref[place] = whole[block, :].astype(jnp.bfloat16)


def after(value, *others):
    return lax.optimization_barrier((value,) + others)[0]


def call(kernel, outs, specs, *operands, scratch=(), steps=0):
    many = isinstance(outs, tuple)
    cost = pl.CostEstimate(flops=steps * 4_000_000_000, bytes_accessed=0, transcendentals=0)
    with jax.named_scope(kernel.__name__):
        return pl.pallas_call(
            kernel,
            out_shape=outs,
            in_specs=specs,
            out_specs=(VMEM,) * len(outs) if many else VMEM,
            scratch_shapes=scratch,
            compiler_params=PARAMS,
            cost_estimate=cost if steps else None,
        )(*operands)


def flipped(value, by):
    return lax.ppermute(value, "mp", [(i, i ^ by) for i in range(lax.axis_size("mp"))])


def on_device(queries, keys, values, out_weight, grad_out, alignment):
    queries, keys, values, grad_out = queries.T, keys.T, values.T, grad_out.T
    feats, frames = keys.shape
    tokens = queries.shape[1]
    heads = feats // DH
    me = lax.axis_index("mp").astype(jnp.int32).reshape(1)
    place = (lax.axis_index("seq").astype(jnp.int32) * (frames // BLK)).reshape(1)
    bf16, f32 = jnp.bfloat16, jnp.float32
    shape = jax.ShapeDtypeStruct

    grad_far = flipped(grad_out, 2)
    frame_pack = call(
        pack_frames,
        shape((heads, PAIR, frames), bf16),
        [HBM] * 2,
        keys,
        values,
        scratch=[pltpu.SemaphoreType.DMA((2, heads))],
    )
    grad_own = after(grad_out, frame_pack)
    grad_other = flipped(jnp.concatenate([grad_own, grad_far], axis=0), 1)
    later_pack = after(frame_pack, grad_far)
    window = [ring(later_pack, 1), frame_pack, ring(later_pack, -1), ring(frame_pack, -2)]

    token_pack = call(
        pack_tokens,
        shape((heads, PAIR, tokens), bf16),
        [SMEM] + [VMEM] * 5,
        me,
        grad_own,
        grad_far,
        grad_other,
        out_weight,
        queries,
        scratch=[pltpu.VMEM((4 * feats, tokens), bf16)],
    )
    turned_weight = after(out_weight, token_pack).T
    sent_pack = after(token_pack, window[3])
    late_pack = after(token_pack, *window)
    token_packs = [ring(late_pack, 1), ring(sent_pack, -1), ring(late_pack, 2)]

    attended, stats = call(
        forward,
        (shape((feats, tokens), bf16), shape((STAT_ROWS, tokens), f32)),
        [SMEM] * 2 + [VMEM] * 5,
        place,
        after(alignment, turned_weight),
        token_pack,
        *window,
        scratch=[pltpu.VMEM((3, BLK, 4 * frames), f32), pltpu.VMEM((tokens, 128), f32)],
        steps=1,
    )
    sent_stats = after(stats, token_packs[1])
    near_stats = [ring(sent_stats, 1), ring(sent_stats, -1), ring(sent_stats, 2)]

    kept, sent = call(
        project,
        (shape((2, feats, tokens), f32), shape((2, feats, tokens), bf16)),
        [SMEM] + [VMEM] * 2,
        me,
        turned_weight,
        after(attended, near_stats[0]),
        scratch=[pltpu.VMEM((4 * feats, tokens), f32)],
    )
    kept = kept + flipped(sent, 2).astype(f32)
    layer_output = (kept[0] + flipped(kept[1].astype(bf16), 1).astype(f32)).astype(bf16)
    query_grad = call(
        query_side,
        shape((feats, tokens), bf16),
        [SMEM] + [VMEM] * 6,
        place,
        token_pack,
        after(sent_stats, token_packs[0]),
        *window,
        steps=1,
    )
    key_grad, value_grad = call(
        frame_side,
        (shape((feats, frames), bf16),) * 2,
        [SMEM] + [VMEM] * 9,
        place,
        frame_pack,
        token_pack,
        *token_packs,
        after(sent_stats, query_grad),
        *near_stats,
        steps=1,
    )
    return layer_output.T, query_grad.T, key_grad.T, value_grad.T


def solution(mesh):
    return jax.shard_map(
        on_device,
        mesh=mesh,
        in_specs=(
            P("seq", "mp"),
            P("seq", "mp"),
            P("seq", "mp"),
            P("mp", None),
            P("seq", "mp"),
            P("seq", None),
        ),
        out_specs=(P("seq", "mp"), P("seq", "mp"), P("seq", "mp"), P("seq", "mp")),
        check_vma=False,
    )
```

```python
import jax
import jax.numpy as jnp
from jax import lax
from jax.experimental import pallas as pl
from jax.experimental.pallas import tpu as pltpu
from jax.sharding import PartitionSpec as P

DH = 64
BLK = 128
PAIR = 2 * DH
FACTOR = DH ** (-0.5)
LOG2E = 1.4426950408889634
FAR = -1e30
BIAS_ROWS = 16
TERMS = 3
STAT_ROWS = 16
NT = (((1,), (1,)), ((), ()))
NN = (((1,), (0,)), ((), ()))
VMEM = pl.BlockSpec(memory_space=pltpu.VMEM)
SMEM = pl.BlockSpec(memory_space=pltpu.SMEM)
PARAMS = pltpu.CompilerParams(vmem_limit_bytes=20 * 1024 * 1024)


def ring(value, by):
    count = lax.axis_size("seq")
    return lax.ppermute(value, "seq", [(i, (i + by) % count) for i in range(count)])


def dot(first_op, second_op, dims):
    return lax.dot_general(first_op, second_op, dims, preferred_element_type=jnp.float32)


def iota(shape, dim):
    return lax.broadcasted_iota(jnp.int32, shape, dim)


def pack_tokens(me_ref, own_ref, far_ref, other_ref, weight_ref, queries_ref, out_ref, whole):
    feats = own_ref.shape[0]
    parts = (own_ref[...], far_ref[...], other_ref[:feats], other_ref[feats:])
    for part, flip in zip(parts, (0, 2, 1, 3)):
        first = pl.multiple_of((me_ref[0] ^ flip) * feats, feats)
        whole[pl.ds(first, feats), :] = part
    grad = dot(weight_ref[...], whole[...], NN).astype(jnp.bfloat16)
    for head in range(out_ref.shape[0]):
        rows = slice(head * DH, (head + 1) * DH)
        out_ref[head, :DH] = queries_ref[rows]
        out_ref[head, DH:] = grad[rows]


def three_terms(row):
    high = row.astype(jnp.bfloat16).astype(jnp.float32)
    middle = (row - high).astype(jnp.bfloat16).astype(jnp.float32)
    return [high, middle, row - high - middle]


def padded(parts):
    have = sum(p.shape[0] for p in parts)
    zeros = jnp.zeros((DH - have, parts[0].shape[1]), jnp.float32)
    return jnp.concatenate(parts + [zeros], axis=0).astype(jnp.bfloat16)


def turned(parts):
    return jnp.concatenate(parts, axis=0).T


def block_bias(first_block, lower, upper):
    block = (first_block + iota((BIAS_ROWS, lower.shape[1]), 0)).astype(jnp.float32)
    return jnp.where((lower <= block) & (block < upper), 0.0, FAR)


def score_rows(frames, first_row):
    row = iota((DH, frames), 0)
    block = first_row + iota((DH, frames), 1) // BLK
    ones = jnp.where(row == block, 1.0, 0.0)
    minus = (row >= BIAS_ROWS) & (row < BIAS_ROWS + TERMS)
    return jnp.where(minus, -1.0, ones).astype(jnp.bfloat16)


def dprob_rows(frames):
    return jnp.where(iota((DH, frames), 0) < TERMS, -1.0, 0.0).astype(jnp.bfloat16)


def score_side(pair, bias, logsum):
    return turned([pair[:DH], padded([bias] + three_terms(logsum))])


def dprob_side(pair, delta):
    return turned([padded(three_terms(delta)), pair[DH:]])


def forward(place_ref, align_ref, pair_ref, f0, f1, f2, f3, attended_ref, stats_ref, work, sums):
    heads, _, tokens = pair_ref.shape
    slots = (f0, f1, f2, f3)
    span = f0.shape[2]
    lane = iota((1, tokens), 1)
    lower = jnp.where(lane < BLK, align_ref[0, 0], align_ref[1, 0]).astype(jnp.float32)
    upper = jnp.where(lane < BLK, align_ref[0, 1], align_ref[1, 1]).astype(jnp.float32)
    bias = block_bias(place_ref[0] - span // BLK, lower, upper)
    beside = [score_rows(span, s * (span // BLK)) for s in range(4)]
    units = [(head, g) for head in range(heads) for g in range(tokens // BLK)]
    sides = {}

    def scores(unit):
        head, g = units[unit]
        if g == 0:
            sides[head] = turned([pair_ref[head, :DH], padded([bias])])
        left = sides[head][g * BLK : (g + 1) * BLK]
        top = None
        for s, slot in enumerate(slots):
            raw = dot(left, jnp.concatenate([slot[head, :DH], beside[s]], axis=0), NN)
            work[unit % 3, :, s * span : (s + 1) * span] = raw
            for c in range(0, span, 128):
                part = raw[:, c : c + 128]
                top = part if top is None else jnp.maximum(top, part)
        return jnp.max(top, axis=1, keepdims=True)

    ahead = scores(0)
    for unit, (head, g) in enumerate(units):
        top = ahead
        if unit + 1 < len(units):
            ahead = scores(unit + 1)
        total = None
        for s in range(4):
            raw = work[unit % 3, :, s * span : (s + 1) * span]
            prob = jnp.exp2((raw - top) * (LOG2E * FACTOR))
            work[unit % 3, :, s * span : (s + 1) * span] = prob
            for c in range(0, span, 128):
                part = prob[:, c : c + 128]
                total = part if total is None else total + part
        total = jnp.sum(total, axis=1, keepdims=True)
        inverse = 1.0 / total
        cols = slice(g * BLK, (g + 1) * BLK)
        sums[cols, head : head + 1] = top + jnp.log(total) * (1.0 / FACTOR)
        out = None
        for s, slot in enumerate(slots):
            low = (work[unit % 3, :, s * span : (s + 1) * span] * inverse).astype(jnp.bfloat16)
            part = dot(low, slot[head, DH:], NT)
            out = part if out is None else out + part
        low_out = out.T.astype(jnp.bfloat16)
        attended_ref[head * DH : (head + 1) * DH, cols] = low_out
        product = low_out.astype(jnp.float32) * pair_ref[head, DH:, cols].astype(jnp.float32)
        stats_ref[heads + head : heads + head + 1, cols] = jnp.sum(product, axis=0, keepdims=True)
    stats_ref[:heads, :] = sums[...].T[:heads]
    stats_ref[2 * heads : 2 * heads + 1, :] = lower
    stats_ref[2 * heads + 1 : 2 * heads + 2, :] = upper
    stats_ref[2 * heads + 2 :, :] = jnp.zeros((STAT_ROWS - 2 * heads - 2, tokens), jnp.float32)


def stat_rows(stats_ref, heads, head):
    return stats_ref[head : head + 1, :], stats_ref[heads + head : heads + head + 1, :]


def span_bias(stats_ref, heads, first_block):
    lower, upper = stats_ref[2 * heads : 2 * heads + 1, :], stats_ref[2 * heads + 1 : 2 * heads + 2, :]
    return block_bias(first_block, lower, upper)


def query_side(place_ref, pair_ref, stats_ref, f0, f1, f2, f3, grad_ref):
    heads, _, tokens = pair_ref.shape
    slots = (f0, f1, f2, f3)
    span = f0.shape[2]
    bias = span_bias(stats_ref, heads, place_ref[0] - span // BLK)
    beside = [score_rows(span, s * (span // BLK)) for s in range(4)]
    above = dprob_rows(span)
    units = [(head, s) for head in range(heads) for s in range(4)]
    sides = {}

    def products(unit):
        head, s = units[unit]
        if s == 0:
            pair = pair_ref[head]
            logsum, delta = stat_rows(stats_ref, heads, head)
            sides[head] = score_side(pair, bias, logsum), dprob_side(pair, delta)
        left, grad_left = sides[head]
        raw = dot(left, jnp.concatenate([slots[s][head, :DH], beside[s]], axis=0), NN)
        return raw, dot(grad_left, jnp.concatenate([above, slots[s][head, DH:]], axis=0), NN)

    ahead = products(0)
    out = None
    for unit, (head, s) in enumerate(units):
        raw, dprob = ahead
        if unit + 1 < len(units):
            ahead = products(unit + 1)
        low = (jnp.exp2(raw * (LOG2E * FACTOR)) * dprob).astype(jnp.bfloat16)
        part = dot(slots[s][head, :DH], low, NT)
        out = part if s == 0 else out + part
        if s == 3:
            rows = slice(head * DH, (head + 1) * DH)
            grad_ref[rows, :] = (out * FACTOR).astype(jnp.bfloat16)


def frame_side(
    place_ref, own_ref, p0, p1, p2, p3, s0, s1, s2, s3, key_grad_ref, value_grad_ref
):
    heads, _, span = own_ref.shape
    sources = ((p0, s0), (p1, s1), (p2, s2), (p3, s3))
    bias = [span_bias(stats, heads, place_ref[0]) for _, stats in sources]
    beside = score_rows(span, 0)
    above = dprob_rows(span)
    units = [(head, j) for head in range(heads) for j in range(len(sources))]

    def products(unit):
        head, j = units[unit]
        right = jnp.concatenate([own_ref[head, :DH], beside], axis=0)
        grad_right = jnp.concatenate([above, own_ref[head, DH:]], axis=0)
        pair = sources[j][0][head]
        logsum, delta = stat_rows(sources[j][1], heads, head)
        raw = dot(score_side(pair, bias[j], logsum), right, NN)
        return raw, dot(dprob_side(pair, delta), grad_right, NN)

    ahead = products(0)
    key_out, value_out = None, None
    for unit, (head, j) in enumerate(units):
        raw, dprob = ahead
        if unit + 1 < len(units):
            ahead = products(unit + 1)
        pair_ref = sources[j][0]
        prob = jnp.exp2(raw * (LOG2E * FACTOR))
        key_part = dot(pair_ref[head, :DH], (prob * dprob).astype(jnp.bfloat16), NN)
        value_part = dot(pair_ref[head, DH:], prob.astype(jnp.bfloat16), NN)
        key_out = key_part if j == 0 else key_out + key_part
        value_out = value_part if j == 0 else value_out + value_part
        if j == len(sources) - 1:
            rows = slice(head * DH, (head + 1) * DH)
            key_grad_ref[rows, :] = (key_out * FACTOR).astype(jnp.bfloat16)
            value_grad_ref[rows, :] = value_out.astype(jnp.bfloat16)


def project(me_ref, weight_ref, attended_ref, kept_ref, sent_ref, whole):
    feats = attended_ref.shape[0]
    whole[...] = dot(weight_ref[...], attended_ref[...], NN)
    for place, flip in enumerate((0, 1)):
        block = pl.ds(pl.multiple_of((me_ref[0] ^ flip) * feats, feats), feats)
        kept_ref[place] = whole[block, :]
    for place, flip in enumerate((2, 3)):
        block = pl.ds(pl.multiple_of((me_ref[0] ^ flip) * feats, feats), feats)
        sent_ref[place] = whole[block, :].astype(jnp.bfloat16)


def after(value, *others):
    return lax.optimization_barrier((value,) + others)[0]


def call(kernel, outs, specs, *operands, scratch=(), steps=0):
    many = isinstance(outs, tuple)
    cost = pl.CostEstimate(flops=steps * 4_000_000_000, bytes_accessed=0, transcendentals=0)
    with jax.named_scope(kernel.__name__):
        return pl.pallas_call(
            kernel,
            out_shape=outs,
            in_specs=specs,
            out_specs=(VMEM,) * len(outs) if many else VMEM,
            scratch_shapes=scratch,
            compiler_params=PARAMS,
            cost_estimate=cost if steps else None,
        )(*operands)


def flipped(value, by):
    return lax.ppermute(value, "mp", [(i, i ^ by) for i in range(lax.axis_size("mp"))])


def on_device(queries, keys, values, out_weight, grad_out, alignment):
    queries, keys, values, grad_out = queries.T, keys.T, values.T, grad_out.T
    feats, frames = keys.shape
    tokens = queries.shape[1]
    heads = feats // DH
    me = lax.axis_index("mp").astype(jnp.int32).reshape(1)
    place = (lax.axis_index("seq").astype(jnp.int32) * (frames // BLK)).reshape(1)
    bf16, f32 = jnp.bfloat16, jnp.float32
    shape = jax.ShapeDtypeStruct

    grad_far = flipped(grad_out, 2)
    frame_pack = jnp.concatenate(
        [keys.reshape(heads, DH, frames), values.reshape(heads, DH, frames)], axis=1
    )
    grad_own = after(grad_out, frame_pack)
    grad_other = flipped(jnp.concatenate([grad_own, grad_far], axis=0), 1)
    later_pack = after(frame_pack, grad_far)
    window = [ring(later_pack, 1), frame_pack, ring(later_pack, -1), ring(frame_pack, -2)]

    token_pack = call(
        pack_tokens,
        shape((heads, PAIR, tokens), bf16),
        [SMEM] + [VMEM] * 5,
        me,
        grad_own,
        grad_far,
        grad_other,
        out_weight,
        queries,
        scratch=[pltpu.VMEM((4 * feats, tokens), bf16)],
    )
    turned_weight = after(out_weight, token_pack).T
    sent_pack = after(token_pack, window[3])
    late_pack = after(token_pack, *window)
    token_packs = [ring(late_pack, 1), ring(sent_pack, -1), ring(late_pack, 2)]

    attended, stats = call(
        forward,
        (shape((feats, tokens), bf16), shape((STAT_ROWS, tokens), f32)),
        [SMEM] * 2 + [VMEM] * 5,
        place,
        after(alignment, turned_weight),
        token_pack,
        *window,
        scratch=[pltpu.VMEM((3, BLK, 4 * frames), f32), pltpu.VMEM((tokens, 128), f32)],
        steps=1,
    )
    sent_stats = after(stats, token_packs[1])
    near_stats = [ring(sent_stats, 1), ring(sent_stats, -1), ring(sent_stats, 2)]

    kept, sent = call(
        project,
        (shape((2, feats, tokens), f32), shape((2, feats, tokens), bf16)),
        [SMEM] + [VMEM] * 2,
        me,
        turned_weight,
        after(attended, near_stats[0]),
        scratch=[pltpu.VMEM((4 * feats, tokens), f32)],
    )
    kept = kept + flipped(sent, 2).astype(f32)
    layer_output = (kept[0] + flipped(kept[1].astype(bf16), 1).astype(f32)).astype(bf16)
    query_grad = call(
        query_side,
        shape((feats, tokens), bf16),
        [SMEM] + [VMEM] * 6,
        place,
        token_pack,
        after(sent_stats, token_packs[0]),
        *window,
        steps=1,
    )
    key_grad, value_grad = call(
        frame_side,
        (shape((feats, frames), bf16),) * 2,
        [SMEM] + [VMEM] * 9,
        place,
        frame_pack,
        token_pack,
        *token_packs,
        after(sent_stats, query_grad),
        *near_stats,
        steps=1,
    )
    return layer_output.T, query_grad.T, key_grad.T, value_grad.T


def solution(mesh):
    return jax.shard_map(
        on_device,
        mesh=mesh,
        in_specs=(
            P("seq", "mp"),
            P("seq", "mp"),
            P("seq", "mp"),
            P("mp", None),
            P("seq", "mp"),
            P("seq", None),
        ),
        out_specs=(P("seq", "mp"), P("seq", "mp"), P("seq", "mp"), P("seq", "mp")),
        check_vma=False,
    )
```

```python
import jax
import jax.numpy as jnp
from jax import lax
from jax.experimental import pallas as pl
from jax.experimental.pallas import tpu as pltpu
from jax.sharding import PartitionSpec as P

DH = 64
BLK = 128
PAIR = 2 * DH
FACTOR = DH ** (-0.5)
LOG2E = 1.4426950408889634
FAR = -1e30
BIAS_ROWS = 16
TERMS = 3
STAT_ROWS = 16
NT = (((1,), (1,)), ((), ()))
NN = (((1,), (0,)), ((), ()))
VMEM = pl.BlockSpec(memory_space=pltpu.VMEM)
SMEM = pl.BlockSpec(memory_space=pltpu.SMEM)
PARAMS = pltpu.CompilerParams(vmem_limit_bytes=20 * 1024 * 1024)


def ring(value, by):
    count = lax.axis_size("seq")
    return lax.ppermute(value, "seq", [(i, (i + by) % count) for i in range(count)])


def dot(first_op, second_op, dims):
    return lax.dot_general(first_op, second_op, dims, preferred_element_type=jnp.float32)


def iota(shape, dim):
    return lax.broadcasted_iota(jnp.int32, shape, dim)


def pack_tokens(me_ref, own_ref, far_ref, other_ref, weight_ref, queries_ref, out_ref, whole):
    feats = own_ref.shape[0]
    parts = (own_ref[...], far_ref[...], other_ref[:feats], other_ref[feats:])
    for part, flip in zip(parts, (0, 2, 1, 3)):
        first = pl.multiple_of((me_ref[0] ^ flip) * feats, feats)
        whole[pl.ds(first, feats), :] = part
    grad = dot(weight_ref[...], whole[...], NN).astype(jnp.bfloat16)
    for head in range(out_ref.shape[0]):
        rows = slice(head * DH, (head + 1) * DH)
        out_ref[head, :DH] = queries_ref[rows]
        out_ref[head, DH:] = grad[rows]


def three_terms(row):
    high = row.astype(jnp.bfloat16).astype(jnp.float32)
    middle = (row - high).astype(jnp.bfloat16).astype(jnp.float32)
    return [high, middle, row - high - middle]


def padded(parts):
    have = sum(p.shape[0] for p in parts)
    zeros = jnp.zeros((DH - have, parts[0].shape[1]), jnp.float32)
    return jnp.concatenate(parts + [zeros], axis=0).astype(jnp.bfloat16)


def turned(parts):
    return jnp.concatenate(parts, axis=0).T


def block_bias(first_block, lower, upper):
    block = (first_block + iota((BIAS_ROWS, lower.shape[1]), 0)).astype(jnp.float32)
    return jnp.where((lower <= block) & (block < upper), 0.0, FAR)


def score_rows(frames, first_row):
    row = iota((DH, frames), 0)
    block = first_row + iota((DH, frames), 1) // BLK
    ones = jnp.where(row == block, 1.0, 0.0)
    minus = (row >= BIAS_ROWS) & (row < BIAS_ROWS + TERMS)
    return jnp.where(minus, -1.0, ones).astype(jnp.bfloat16)


def dprob_rows(frames):
    return jnp.where(iota((DH, frames), 0) < TERMS, -1.0, 0.0).astype(jnp.bfloat16)


def score_side(pair, bias, logsum):
    return turned([pair[:DH], padded([bias] + three_terms(logsum))])


def dprob_side(pair, delta):
    return turned([padded(three_terms(delta)), pair[DH:]])


def forward(place_ref, align_ref, pair_ref, f0, f1, f2, f3, attended_ref, stats_ref, work, sums):
    heads, _, tokens = pair_ref.shape
    slots = (f0, f1, f2, f3)
    span = f0.shape[2]
    lane = iota((1, tokens), 1)
    lower = jnp.where(lane < BLK, align_ref[0, 0], align_ref[1, 0]).astype(jnp.float32)
    upper = jnp.where(lane < BLK, align_ref[0, 1], align_ref[1, 1]).astype(jnp.float32)
    bias = block_bias(place_ref[0] - span // BLK, lower, upper)
    beside = [score_rows(span, s * (span // BLK)) for s in range(4)]
    units = [(head, g) for head in range(heads) for g in range(tokens // BLK)]
    sides = {}

    def scores(unit):
        head, g = units[unit]
        if g == 0:
            sides[head] = turned([pair_ref[head, :DH], padded([bias])])
        left = sides[head][g * BLK : (g + 1) * BLK]
        top = None
        for s, slot in enumerate(slots):
            raw = dot(left, jnp.concatenate([slot[head, :DH], beside[s]], axis=0), NN)
            work[unit % 3, :, s * span : (s + 1) * span] = raw
            for c in range(0, span, 128):
                part = raw[:, c : c + 128]
                top = part if top is None else jnp.maximum(top, part)
        return jnp.max(top, axis=1, keepdims=True)

    ahead = scores(0)
    for unit, (head, g) in enumerate(units):
        top = ahead
        if unit + 1 < len(units):
            ahead = scores(unit + 1)
        total = None
        for s in range(4):
            raw = work[unit % 3, :, s * span : (s + 1) * span]
            prob = jnp.exp2((raw - top) * (LOG2E * FACTOR))
            work[unit % 3, :, s * span : (s + 1) * span] = prob
            for c in range(0, span, 128):
                part = prob[:, c : c + 128]
                total = part if total is None else total + part
        total = jnp.sum(total, axis=1, keepdims=True)
        inverse = 1.0 / total
        cols = slice(g * BLK, (g + 1) * BLK)
        sums[cols, head : head + 1] = top + jnp.log(total) * (1.0 / FACTOR)
        out = None
        for s, slot in enumerate(slots):
            low = (work[unit % 3, :, s * span : (s + 1) * span] * inverse).astype(jnp.bfloat16)
            part = dot(low, slot[head, DH:], NT)
            out = part if out is None else out + part
        low_out = out.T.astype(jnp.bfloat16)
        attended_ref[head * DH : (head + 1) * DH, cols] = low_out
        product = low_out.astype(jnp.float32) * pair_ref[head, DH:, cols].astype(jnp.float32)
        stats_ref[heads + head : heads + head + 1, cols] = jnp.sum(product, axis=0, keepdims=True)
    stats_ref[:heads, :] = sums[...].T[:heads]
    stats_ref[2 * heads : 2 * heads + 1, :] = lower
    stats_ref[2 * heads + 1 : 2 * heads + 2, :] = upper
    stats_ref[2 * heads + 2 :, :] = jnp.zeros((STAT_ROWS - 2 * heads - 2, tokens), jnp.float32)


def stat_rows(stats_ref, heads, head):
    return stats_ref[head : head + 1, :], stats_ref[heads + head : heads + head + 1, :]


def span_bias(stats_ref, heads, first_block):
    lower, upper = stats_ref[2 * heads : 2 * heads + 1, :], stats_ref[2 * heads + 1 : 2 * heads + 2, :]
    return block_bias(first_block, lower, upper)


def query_side(place_ref, pair_ref, stats_ref, f0, f1, f2, f3, grad_ref):
    heads, _, tokens = pair_ref.shape
    slots = (f0, f1, f2, f3)
    span = f0.shape[2]
    bias = span_bias(stats_ref, heads, place_ref[0] - span // BLK)
    beside = [score_rows(span, s * (span // BLK)) for s in range(4)]
    above = dprob_rows(span)
    units = [(head, s) for head in range(heads) for s in range(4)]
    sides = {}

    def products(unit):
        head, s = units[unit]
        if s == 0:
            pair = pair_ref[head]
            logsum, delta = stat_rows(stats_ref, heads, head)
            sides[head] = score_side(pair, bias, logsum), dprob_side(pair, delta)
        left, grad_left = sides[head]
        raw = dot(left, jnp.concatenate([slots[s][head, :DH], beside[s]], axis=0), NN)
        return raw, dot(grad_left, jnp.concatenate([above, slots[s][head, DH:]], axis=0), NN)

    ahead = products(0)
    out = None
    for unit, (head, s) in enumerate(units):
        raw, dprob = ahead
        if unit + 1 < len(units):
            ahead = products(unit + 1)
        low = (jnp.exp2(raw * (LOG2E * FACTOR)) * dprob).astype(jnp.bfloat16)
        part = dot(slots[s][head, :DH], low, NT)
        out = part if s == 0 else out + part
        if s == 3:
            rows = slice(head * DH, (head + 1) * DH)
            grad_ref[rows, :] = (out * FACTOR).astype(jnp.bfloat16)


def frame_side(
    place_ref, own_ref, p0, p1, p2, p3, s0, s1, s2, s3, key_grad_ref, value_grad_ref
):
    heads, _, span = own_ref.shape
    sources = ((p0, s0), (p1, s1), (p2, s2), (p3, s3))
    bias = [span_bias(stats, heads, place_ref[0]) for _, stats in sources]
    beside = score_rows(span, 0)
    above = dprob_rows(span)
    units = [(head, j) for head in range(heads) for j in range(len(sources))]

    def products(unit):
        head, j = units[unit]
        right = jnp.concatenate([own_ref[head, :DH], beside], axis=0)
        grad_right = jnp.concatenate([above, own_ref[head, DH:]], axis=0)
        pair = sources[j][0][head]
        logsum, delta = stat_rows(sources[j][1], heads, head)
        raw = dot(score_side(pair, bias[j], logsum), right, NN)
        return raw, dot(dprob_side(pair, delta), grad_right, NN)

    ahead = products(0)
    key_out, value_out = None, None
    for unit, (head, j) in enumerate(units):
        raw, dprob = ahead
        if unit + 1 < len(units):
            ahead = products(unit + 1)
        pair_ref = sources[j][0]
        prob = jnp.exp2(raw * (LOG2E * FACTOR))
        key_part = dot(pair_ref[head, :DH], (prob * dprob).astype(jnp.bfloat16), NN)
        value_part = dot(pair_ref[head, DH:], prob.astype(jnp.bfloat16), NN)
        key_out = key_part if j == 0 else key_out + key_part
        value_out = value_part if j == 0 else value_out + value_part
        if j == len(sources) - 1:
            rows = slice(head * DH, (head + 1) * DH)
            key_grad_ref[rows, :] = (key_out * FACTOR).astype(jnp.bfloat16)
            value_grad_ref[rows, :] = value_out.astype(jnp.bfloat16)


def project(me_ref, weight_ref, attended_ref, kept_ref, sent_ref, whole):
    feats = attended_ref.shape[0]
    whole[...] = dot(weight_ref[...], attended_ref[...], NN)
    for place, flip in enumerate((0, 1)):
        block = pl.ds(pl.multiple_of((me_ref[0] ^ flip) * feats, feats), feats)
        kept_ref[place] = whole[block, :]
    for place, flip in enumerate((2, 3)):
        block = pl.ds(pl.multiple_of((me_ref[0] ^ flip) * feats, feats), feats)
        sent_ref[place] = whole[block, :].astype(jnp.bfloat16)


def after(value, *others):
    return lax.optimization_barrier((value,) + others)[0]


def call(kernel, outs, specs, *operands, scratch=(), steps=0):
    many = isinstance(outs, tuple)
    cost = pl.CostEstimate(flops=steps * 4_000_000_000, bytes_accessed=0, transcendentals=0)
    with jax.named_scope(kernel.__name__):
        return pl.pallas_call(
            kernel,
            out_shape=outs,
            in_specs=specs,
            out_specs=(VMEM,) * len(outs) if many else VMEM,
            scratch_shapes=scratch,
            compiler_params=PARAMS,
            cost_estimate=cost if steps else None,
        )(*operands)


def flipped(value, by):
    return lax.ppermute(value, "mp", [(i, i ^ by) for i in range(lax.axis_size("mp"))])


def on_device(queries, keys, values, out_weight, grad_out, alignment):
    queries, keys, values, grad_out = queries.T, keys.T, values.T, grad_out.T
    feats, frames = keys.shape
    tokens = queries.shape[1]
    heads = feats // DH
    me = lax.axis_index("mp").astype(jnp.int32).reshape(1)
    place = (lax.axis_index("seq").astype(jnp.int32) * (frames // BLK)).reshape(1)
    bf16, f32 = jnp.bfloat16, jnp.float32
    shape = jax.ShapeDtypeStruct

    grad_far = flipped(grad_out, 2)
    frame_pack = jnp.concatenate(
        [keys.reshape(heads, DH, frames), values.reshape(heads, DH, frames)], axis=1
    )
    grad_own = after(grad_out, frame_pack)
    grad_other = flipped(jnp.concatenate([grad_own, grad_far], axis=0), 1)
    later_pack = after(frame_pack, grad_far)
    window = [ring(later_pack, 1), frame_pack, ring(later_pack, -1), ring(frame_pack, -2)]

    token_pack = call(
        pack_tokens,
        shape((heads, PAIR, tokens), bf16),
        [SMEM] + [VMEM] * 5,
        me,
        grad_own,
        grad_far,
        grad_other,
        out_weight,
        queries,
        scratch=[pltpu.VMEM((4 * feats, tokens), bf16)],
    )
    turned_weight = after(out_weight, token_pack).T
    sent_pack = after(token_pack, window[3])
    late_pack = after(token_pack, *window)
    token_packs = [ring(late_pack, 1), ring(sent_pack, -1), None]

    attended, stats = call(
        forward,
        (shape((feats, tokens), bf16), shape((STAT_ROWS, tokens), f32)),
        [SMEM] * 2 + [VMEM] * 5,
        place,
        after(alignment, turned_weight),
        token_pack,
        *window,
        scratch=[pltpu.VMEM((3, BLK, 4 * frames), f32), pltpu.VMEM((tokens, 128), f32)],
        steps=1,
    )
    sent_stats = after(stats, token_packs[1])
    token_packs[2] = ring(after(token_pack, sent_stats), 2)
    near_stats = [ring(sent_stats, 1), ring(sent_stats, -1), ring(sent_stats, 2)]

    kept, sent = call(
        project,
        (shape((2, feats, tokens), f32), shape((2, feats, tokens), bf16)),
        [SMEM] + [VMEM] * 2,
        me,
        turned_weight,
        after(attended, near_stats[0]),
        scratch=[pltpu.VMEM((4 * feats, tokens), f32)],
    )
    kept = kept + flipped(sent, 2).astype(f32)
    layer_output = (kept[0] + flipped(kept[1].astype(bf16), 1).astype(f32)).astype(bf16)
    query_grad = call(
        query_side,
        shape((feats, tokens), bf16),
        [SMEM] + [VMEM] * 6,
        place,
        token_pack,
        after(sent_stats, token_packs[0]),
        *window,
        steps=1,
    )
    key_grad, value_grad = call(
        frame_side,
        (shape((feats, frames), bf16),) * 2,
        [SMEM] + [VMEM] * 9,
        place,
        frame_pack,
        token_pack,
        *token_packs,
        after(sent_stats, query_grad),
        *near_stats,
        steps=1,
    )
    return layer_output.T, query_grad.T, key_grad.T, value_grad.T


def solution(mesh):
    return jax.shard_map(
        on_device,
        mesh=mesh,
        in_specs=(
            P("seq", "mp"),
            P("seq", "mp"),
            P("seq", "mp"),
            P("mp", None),
            P("seq", "mp"),
            P("seq", None),
        ),
        out_specs=(P("seq", "mp"), P("seq", "mp"), P("seq", "mp"), P("seq", "mp")),
        check_vma=False,
    )
```
